32 devices in a mesh: groups: 2 (over x), width: 16 (over z, y, core).
Axes of the slice: x: 2, y: 2, z: 4, core: 2. Of those that a mesh axis runs over, the one named last changes fastest.
Arguments:
- stream_in: bfloat16 [2, 128, 8192], P(None, 'groups', 'width'), parts along dimension 1, may hold values from -16 to 16
- norm_gain: float32 [2, 8192], replicated, may hold values from 0.1 to 1.9
- w_gate: bfloat16 [2, 8192, 14336], P(None, None, 'width'), may hold values from -0.0625 to 0.0625
- w_up: bfloat16 [2, 8192, 14336], P(None, None, 'width'), may hold values from -0.0625 to 0.0625
- w_down: bfloat16 [2, 14336, 8192], P(None, 'width'), may hold values from -0.0625 to 0.0625
Outputs:
- stream_out: bfloat16 [2, 128, 8192], P(None, 'groups', 'width'), parts along dimension 1
The draws below stay inside these ranges and needn't reach their ends.
There are 2 independent parts, one for each index of `groups`. The reference program is written for one: setup_inputs(seed, part) draws one part's arguments, and reference() takes and returns one part's arrays. A program takes and returns all parts, laid end to end along the dimension named above; an argument that names none is the same for every part. Nothing has to cross between parts.
All inputs are finite; a program needn't handle non-finite values.
Results may differ from the reference program's by a relative error of at most 0.012.
Values may be sent and summed in bfloat16 or wider, within the bound.
No kernel may reach another device: no remote copies, remote signals or barrier semaphores. Data moves between devices by JAX's collectives and lax.ppermute only.
A program may use at most 192 MiB of HBM per device.

```python
import math
import jax
import jax.numpy as jnp
from jax import lax

D = 8192
FF = 14336
LAYERS = 2
MICRO = 2
ROWS = 64


def draw_stream_in(key, part):
    key_base, key_column, key_row = jax.random.split(key, 3)
    column_pos = jnp.arange(D, dtype=jnp.float32) / (D - 1)
    column_scale = 3.0 ** column_pos / 3.0 * jnp.exp(jax.random.uniform(key_column, (D,), jnp.float32, math.log(0.55), math.log(1.8)))
    base_values = jax.random.normal(key_base, (MICRO, ROWS, D), jnp.float32)
    row_scale = jnp.exp(jax.random.uniform(key_row, (MICRO, ROWS, 1), jnp.float32, math.log(0.3), math.log(3.0)))
    values = jnp.clip(base_values * row_scale * column_scale, -16.0, 16.0)
    return values.astype(jnp.bfloat16)


def with_spikes(array, key, source, target, parts, factor):
    owner, partner = [(jnp.arange(array.shape[dim]) // (array.shape[dim] // parts)).reshape([-1 if axis == dim else 1 for axis in range(array.ndim)]) for dim in (source, target)]
    chosen = jax.random.permutation(key, parts)[partner]
    strong = (owner == chosen) | (owner == (partner + parts // 2) % parts)
    return jnp.where(strong, factor * array, array)


def level_of(stream_key, extent, shards, smallest, top_value):
    def one(position, blocks):
        draws = jax.random.uniform(jax.random.fold_in(jax.random.fold_in(stream_key, 6), position), (blocks,), jnp.float32, smallest / len(shards), top_value / len(shards))
        return jnp.repeat(jnp.exp(draws), extent[position] // blocks).reshape((-1,) + (1,) * (len(extent) - position - 1))

    factor_of = one(*shards[0])
    for cut in shards[1:]:
        factor_of = factor_of * one(*cut)
    return factor_of


def bell_draw(key, extent, width, limit, cuts=(), kind=jnp.bfloat16):
    drawn = width * jax.random.normal(key, extent, jnp.float32)
    if cuts:
        drawn = drawn * level_of(key, extent, cuts, -0.22, 0.18)
    return jnp.clip(drawn, -limit, limit).astype(kind)


def bell_draw_with(key, shape, deviation, limit, pieces, heavy, kind=jnp.bfloat16):
    values = deviation * jax.random.normal(key, shape, jnp.float32)
    if pieces:
        values = values * level_of(key, shape, pieces, -0.22, 0.18)
    return jnp.clip(with_spikes(values, jax.random.fold_in(key, 3), *heavy), -limit, limit).astype(kind)


def setup_inputs(seed: int = 0, part: int = 0) -> dict:
    seeds = jax.random.split(jax.random.key(seed), 6)
    own_keys = jax.random.split(jax.random.fold_in(seeds[5], part), 6)
    stream_in = draw_stream_in(jax.random.fold_in(jax.random.fold_in(seeds[5], part), 71), part)
    norm_gain = jnp.clip(1.0 + 0.18 * jax.random.normal(seeds[1], (LAYERS, D), jnp.float32), 0.1, 1.9)
    w_gate = bell_draw(seeds[2], (LAYERS, D, FF), D ** -0.5, 0.0625, ((2, 16),))
    w_up = bell_draw(seeds[3], (LAYERS, D, FF), D ** -0.5, 0.0625, ((2, 16),))
    w_down = bell_draw_with(seeds[4], (LAYERS, FF, D), FF ** -0.5, 0.0625, ((1, 16),), (1, 2, 16, 2.0))
    return dict(stream_in=stream_in, norm_gain=norm_gain, w_gate=w_gate, w_up=w_up, w_down=w_down)


def sublayer(stream, gain_row, gate_weight, up_weight, down_weight):
    stream_f = stream.astype(jnp.float32)
    meansq = lax.optimization_barrier(jnp.mean(stream_f * stream_f, axis=1, keepdims=True))
    normed = (stream_f * lax.rsqrt(meansq + 1e-05) * gain_row).astype(jnp.bfloat16)
    gate_out = jnp.dot(normed, gate_weight, preferred_element_type=jnp.float32)
    up_out = jnp.dot(normed, up_weight, preferred_element_type=jnp.float32)
    hidden = (jax.nn.silu(gate_out) * up_out).astype(jnp.bfloat16)
    branch = jnp.dot(hidden, down_weight, preferred_element_type=jnp.float32)
    return (stream_f + branch).astype(jnp.bfloat16)

def reference(stream_in, norm_gain, w_gate, w_up, w_down):
    results = []
    for micro_index in range(MICRO):
        stream = stream_in[micro_index]
        for depth in range(LAYERS):
            stream = sublayer(stream, norm_gain[depth], w_gate[depth], w_up[depth], w_down[depth])
        results.append(stream)
    return jnp.stack(results)
```

```python
import functools

import jax
import jax.numpy as jnp
from jax import lax
from jax.experimental import pallas as pl
from jax.experimental.pallas import tpu as pltpu
from jax.sharding import PartitionSpec as P

AXIS = "width"
EPS = 1e-05
VMEM = pl.BlockSpec(memory_space=pltpu.VMEM)
HBM = pl.BlockSpec(memory_space=pl.ANY)
LIMIT = 40 * 1024 * 1024


def place_of(chip, chips):
    half = chip // 2
    odd = chip - 2 * half
    return half + odd * (chips - 1 - 2 * half)


def chip_at(place, chips):
    far = (place >= chips // 2) * 1
    return 2 * place + far * (2 * chips - 1 - 4 * place)


def shard_at(offset, sibling, chips):
    me = lax.axis_index(AXIS)
    chip = me // 2
    core = me - 2 * chip
    place = lax.rem(place_of(chip, chips) + (offset + chips), chips)
    far = jnp.where(place >= chips // 2, 1, 0)
    there = 2 * place + far * (2 * chips - 1 - 4 * place)
    return 2 * there + (1 - core if sibling else core)


def gate_up_kernel(layer, chips, plan, first, last, *refs):
    refs = list(refs)
    gain_ref, wg_hbm, wu_hbm = refs[:3]
    at = 3
    xs = []
    for _, _, pieces in plan:
        xs.append(refs[at : at + pieces])
        at += pieces
    if not first:
        g_in, u_in, q_in = refs[at : at + 3]
        at += 3
    if last:
        hid_ref = refs[at]
        at += 1
        g_ref, u_ref, q_ref, wg, wu, sems = refs[at:]
    else:
        g_ref, u_ref, q_ref, wg, wu, sems = refs[at:]
    depth = wg.shape[1]
    ids = [shard_at(offset, sibling, chips) for offset, sibling, _ in plan]
    copies = []
    for e, shard in enumerate(ids):
        rows = pl.ds(pl.multiple_of(shard * depth, depth), depth)
        pair = (
            pltpu.make_async_copy(wg_hbm.at[layer, rows, :], wg.at[e], sems.at[e, 0]),
            pltpu.make_async_copy(wu_hbm.at[layer, rows, :], wu.at[e], sems.at[e, 1]),
        )
        for copy in pair:
            copy.start()
        copies.append(pair)
    for e, shard in enumerate(ids):
        parts = [ref[...] for ref in xs[e]]
        x = (parts[0] if len(parts) == 1 else jnp.concatenate(parts, 0)).astype(jnp.float32)
        square = x * x
        q = square[:, :128]
        for lane in range(128, depth, 128):
            q = q + square[:, lane : lane + 128]
        y = (x * gain_ref[layer, shard]).astype(jnp.bfloat16)
        copies[e][0].wait()
        g = jnp.dot(y, wg[e], preferred_element_type=jnp.float32)
        copies[e][1].wait()
        u = jnp.dot(y, wu[e], preferred_element_type=jnp.float32)
        if e == 0 and first:
            g_ref[...], u_ref[...], q_ref[...] = g, u, q
        elif e == 0:
            g_ref[...], u_ref[...], q_ref[...] = g_in[...] + g, u_in[...] + u, q_in[...] + q
        else:
            g_ref[...] += g
            u_ref[...] += u
            q_ref[...] += q
    if last:
        features = depth * 2 * chips
        meansq = jnp.sum(q_ref[...], axis=1, keepdims=True) / features
        scale = lax.rsqrt(meansq + EPS)
        g = g_ref[...] * scale
        hid_ref[...] = (g / (1.0 + jnp.exp(-g)) * (u_ref[...] * scale)).astype(jnp.bfloat16)


def gate_up(layer, chips, plan, xs, gain, wg, wu, acc, last):
    depth = xs[0].shape[-1]
    hid = wg.shape[2]
    rows = 128 if not isinstance(xs[0], tuple) else 0
    rows = max(x.shape[0] for x in xs)
    if all(p[2] == 2 for p in plan):
        rows = 2 * xs[0].shape[0]
    k = len(plan)
    f32 = jnp.float32
    sums = [
        jax.ShapeDtypeStruct((rows, hid), f32),
        jax.ShapeDtypeStruct((rows, hid), f32),
        jax.ShapeDtypeStruct((rows, 128), f32),
    ]
    scratch = [
        pltpu.VMEM((k, depth, hid), jnp.bfloat16),
        pltpu.VMEM((k, depth, hid), jnp.bfloat16),
        pltpu.SemaphoreType.DMA((k, 2)),
    ]
    n_in = 3 + len(xs) + (3 if acc else 0)
    if last:
        out_shape = jax.ShapeDtypeStruct((rows, hid), jnp.bfloat16)
        out_specs = VMEM
        scratch = [pltpu.VMEM(s.shape, s.dtype) for s in sums] + scratch
        aliases = {}
    else:
        out_shape = sums
        out_specs = [VMEM] * 3
        aliases = {3 + len(xs) + i: i for i in range(3)} if acc else {}
    return pl.pallas_call(
        functools.partial(gate_up_kernel, layer, chips, plan, not acc, last),
        out_shape=out_shape,
        in_specs=[VMEM, HBM, HBM] + [VMEM] * (n_in - 3),
        out_specs=out_specs,
        scratch_shapes=scratch,
        input_output_aliases=aliases,
        compiler_params=pltpu.CompilerParams(vmem_limit_bytes=LIMIT),
        cost_estimate=pl.CostEstimate(
            flops=4 * k * rows * depth * hid, bytes_accessed=4 * k * depth * hid, transcendentals=0
        ),
        name="gate_up",
    )(gain, wg, wu, *xs, *(acc or ()))


def down_kernel(layer, chips, offsets, hid_ref, w_hbm, *refs):
    k = len(offsets)
    own, sib = refs[:k], refs[k : 2 * k]
    w, sems = refs[2 * k :]
    cols = w.shape[3]
    copies = []
    for e, offset in enumerate(offsets):
        pair = []
        for side in (1, 0):
            start = pl.multiple_of(shard_at(offset, side == 1, chips) * cols, cols)
            pair.append(
                pltpu.make_async_copy(w_hbm.at[layer, :, pl.ds(start, cols)], w.at[e, side], sems.at[e, side])
            )
            pair[-1].start()
        copies.append(pair)
    for e in range(k):
        copies[e][0].wait()
        sib[e][...] = jnp.dot(hid_ref[...], w[e, 1], preferred_element_type=jnp.float32).astype(jnp.bfloat16)
        copies[e][1].wait()
        own[e][...] = jnp.dot(hid_ref[...], w[e, 0], preferred_element_type=jnp.float32)


def down(layer, chips, offsets, hidden, wd, cols):
    k = len(offsets)
    rows, hid = hidden.shape
    outs = pl.pallas_call(
        functools.partial(down_kernel, layer, chips, offsets),
        out_shape=[jax.ShapeDtypeStruct((rows, cols), jnp.float32)] * k
        + [jax.ShapeDtypeStruct((rows, cols), jnp.bfloat16)] * k,
        in_specs=[VMEM, HBM],
        out_specs=[VMEM] * (2 * k),
        scratch_shapes=[pltpu.VMEM((k, 2, hid, cols), jnp.bfloat16), pltpu.SemaphoreType.DMA((k, 2))],
        compiler_params=pltpu.CompilerParams(vmem_limit_bytes=LIMIT),
        cost_estimate=pl.CostEstimate(
            flops=4 * k * rows * cols * hid, bytes_accessed=4 * k * cols * hid, transcendentals=0
        ),
        name="down",
    )(hidden, wd)
    return outs[:k], outs[k:]


def ring_body(chips, stream_in, norm_gain, w_gate, w_up, w_down):
    micro, seqs, cols = stream_in.shape
    rows = micro * seqs
    part = rows // 2
    layers = w_gate.shape[0]
    far = chips // 2
    ring = [chip_at(place, chips) for place in range(chips)]
    right = [(2 * ring[i] + c, 2 * ring[(i + 1) % chips] + c) for i in range(chips) for c in range(2)]
    left = [(b, a) for a, b in right]
    core = [(i, i ^ 1) for i in range(2 * chips)]

    def send(x, perm):
        return lax.ppermute(x, AXIS, perm)

    f32, bf16 = jnp.float32, jnp.bfloat16
    gain = norm_gain.reshape(layers, 2 * chips, 1, cols)
    stream = stream_in.reshape(rows, cols)
    for layer in range(layers):
        args = (gain, w_gate, w_up)
        r = l = stream
        acc = None
        ready = [(0, False, 1, (stream,))]
        crossing = [(0, send(stream, core))]
        for step in range(1, far):
            r, l = send(r, right), send(l, left)
            acc = gate_up(layer, chips, [e[:3] for e in ready], [x for e in ready for x in e[3]], *args, acc, False)
            ready = [(o, True, 1, (x,)) for o, x in crossing] + [(-step, False, 1, (r,)), (step, False, 1, (l,))]
            crossing = [(-step, send(r, core)), (step, send(l, core))]
        r, l = send(r[:part], right), send(l[part:], left)
        acc = gate_up(layer, chips, [e[:3] for e in ready], [x for e in ready for x in e[3]], *args, acc, False)
        ready = [(o, True, 1, (x,)) for o, x in crossing] + [(far, False, 2, (r, l))]
        rc, lc = send(r, core), send(l, core)
        acc = gate_up(layer, chips, [e[:3] for e in ready], [x for e in ready for x in e[3]], *args, acc, False)
        hidden = gate_up(layer, chips, [(far, True, 2)], [rc, lc], *args, acc, True)
        (own,), (sib,) = down(layer, chips, [far], hidden, w_down, cols)
        total = own + send(sib, core).astype(f32)
        total = total.astype(bf16)
        r, l = send(total[:part], right), send(total[part:], left)
        for step in range(far - 1, 0, -1):
            own, sib = down(layer, chips, [step, -step], hidden, w_down, cols)
            cross = [send(s, core).astype(f32) for s in sib]
            sums = [own[0] + cross[0], own[1] + cross[1]]
            if step == far - 1:
                hole = jnp.zeros((part, cols), bf16)
                r = jnp.concatenate([r, hole], 0)
                l = jnp.concatenate([hole, l], 0)
            r = send((sums[0] + r.astype(f32)).astype(bf16), right)
            l = send((sums[1] + l.astype(f32)).astype(bf16), left)
        (own,), (sib,) = down(layer, chips, [0], hidden, w_down, cols)
        branch = own + send(sib, core).astype(f32)
        stream = (stream.astype(f32) + branch + r.astype(f32) + l.astype(f32)).astype(bf16)
    return stream.reshape(micro, seqs, cols)


def plain_body(stream_in, norm_gain, w_gate, w_up, w_down):
    micro, seqs, cols = stream_in.shape
    layers = w_gate.shape[0]
    f32, bf16 = jnp.float32, jnp.bfloat16
    stream = stream_in.reshape(micro * seqs, cols)
    for layer in range(layers):
        whole = lax.all_gather(stream, AXIS, axis=1, tiled=True).astype(f32)
        meansq = jnp.mean(whole * whole, axis=1, keepdims=True)
        normed = (whole * lax.rsqrt(meansq + EPS) * norm_gain[layer]).astype(bf16)
        gate_out = jnp.dot(normed, w_gate[layer], preferred_element_type=f32)
        up_out = jnp.dot(normed, w_up[layer], preferred_element_type=f32)
        hidden = (jax.nn.silu(gate_out) * up_out).astype(bf16)
        partials = jnp.dot(hidden, w_down[layer], preferred_element_type=f32)
        branch = lax.psum_scatter(partials, AXIS, scatter_dimension=1, tiled=True)
        stream = (stream.astype(f32) + branch).astype(bf16)
    return stream.reshape(micro, seqs, cols)


def solution(mesh):
    devices = mesh.shape[AXIS]

    def body(stream_in, *rest):
        cols = stream_in.shape[2]
        if devices % 8 == 0 and cols % 128 == 0:
            return ring_body(devices // 2, stream_in, *rest)
        return plain_body(stream_in, *rest)

    return jax.shard_map(
        body,
        mesh=mesh,
        in_specs=(
            P(None, "groups", AXIS),
            P(),
            P(None, None, AXIS),
            P(None, None, AXIS),
            P(None, AXIS, None),
        ),
        out_specs=P(None, "groups", AXIS),
        check_vma=False,
    )
```

```python
import functools

import jax
import jax.numpy as jnp
from jax import lax
from jax.experimental import pallas as pl
from jax.experimental.pallas import tpu as pltpu
from jax.sharding import PartitionSpec as P

AXIS = "width"
EPS = 1e-05
VMEM = pl.BlockSpec(memory_space=pltpu.VMEM)
HBM = pl.BlockSpec(memory_space=pl.ANY)
LIMIT = 20 * 1024 * 1024
DIRECT = ()
AHEAD = {
    (0, "gather1"): 4, (0, "gather2"): 4, (0, "gather3"): 4, (0, "gather4"): 4, (0, "gathered"): 2,
    (0, "scatter2"): 2, (0, "scatter1"): 4, (0, "scatter0"): 4,
    (1, "gather1"): 4, (1, "gather2"): 4, (1, "gather3"): 2,
}


def place_of(chip, chips):
    half = chip // 2
    return half + (chip - 2 * half) * (chips - 1 - 2 * half)


def chip_at(place, chips):
    far = (place >= chips // 2) * 1
    return 2 * place + far * (2 * chips - 1 - 4 * place)


def shard_at(offset, sibling, chips):
    me = lax.axis_index(AXIS)
    chip = me // 2
    core = me - 2 * chip
    place = lax.rem(place_of(chip, chips) + (offset + chips), chips)
    far = jnp.where(place >= chips // 2, 1, 0)
    there = 2 * place + far * (2 * chips - 1 - 4 * place)
    return 2 * there + (1 - core if sibling else core)


def view(key, ref, chips):
    kind, layer, offset, sibling = key
    size = ref.shape[2 if kind == "d" else 1] // (2 * chips)
    span = pl.ds(pl.multiple_of(shard_at(offset, sibling, chips) * size, size), size)
    return ref.at[layer, :, span] if kind == "d" else ref.at[layer, span, :]


def stage_kernel(chips, job, raw, stream, fetch, names_in, names_out, *refs):
    named = dict(zip(names_in, refs))
    out = dict(zip(names_out, refs[len(names_in) :]))
    scratch = list(refs[len(names_in) + len(names_out) :])
    copies = {}
    if raw or stream or fetch:
        sems = scratch.pop()
        for e, name in enumerate(raw):
            copies[name] = pltpu.make_async_copy(named["raw", name], out[name], sems.at[len(stream + fetch) + e])
            copies[name].start()
            named[name] = out[name]
        for e, key in enumerate(stream + fetch):
            if key in stream:
                named[key] = scratch.pop(0)
            to = named[key] if key in stream else out[key]
            copies[key] = pltpu.make_async_copy(view(key, named["hbm", key[0]], chips), to, sems.at[e])
            copies[key].start()

    def block(key):
        if key in copies:
            copies[key].wait()
        return named[key][...]

    for name in raw:
        copies[name].wait()
    job(block, named, out, scratch)
    for key in fetch:
        copies[key].wait()


def stage(chips, weights, blocks, job, keys, inputs, outputs, aliases, scratch, ahead, flops, name, raw=()):
    ins = dict(inputs)
    stream = []
    units = [unit for unit in weights["units"] if unit[0] not in keys]
    fetch = [key for unit in units[:ahead] for key in unit]
    weights["units"] = units[ahead:]
    for key in keys:
        if key in blocks:
            ins[key] = blocks.pop(key)
        else:
            stream.append(key)
    _, features, hid = weights["g"].shape
    size = features // (2 * chips)
    shapes = {key: (hid, size) if key[0] == "d" else (size, hid) for key in stream + fetch}
    kinds = sorted({key[0] for key in stream + fetch})
    names_in = list(ins) + [("hbm", kind) for kind in kinds] + [("raw", key) for key in raw]
    out_shape = dict(outputs)
    for key in raw:
        out_shape[key] = jax.ShapeDtypeStruct(raw[key].shape, raw[key].dtype)
    for key in fetch:
        out_shape[key] = jax.ShapeDtypeStruct(shapes[key], jnp.bfloat16)
    names_out = list(out_shape)
    scratch = [pltpu.VMEM(shapes[key], jnp.bfloat16) for key in stream] + scratch
    if raw or stream or fetch:
        scratch.append(pltpu.SemaphoreType.DMA((len(stream + fetch) + len(raw),)))
    results = pl.pallas_call(
        functools.partial(stage_kernel, chips, job, list(raw), stream, fetch, names_in, names_out),
        out_shape=list(out_shape.values()),
        in_specs=[VMEM] * len(ins) + [HBM] * (len(kinds) + len(raw)),
        out_specs=[VMEM] * len(names_out),
        scratch_shapes=scratch,
        input_output_aliases={names_in.index(a): names_out.index(b) for a, b in aliases.items()},
        compiler_params=pltpu.CompilerParams(vmem_limit_bytes=LIMIT),
        cost_estimate=pl.CostEstimate(
            flops=flops, bytes_accessed=sum(2 * a * b for a, b in shapes.values()), transcendentals=0
        ),
        name=name,
    )(
        *ins.values(),
        *(pltpu.with_memory_space_constraint(x, pltpu.HBM) for x in [*(weights[k] for k in kinds), *dict(raw).values()]),
    )
    results = dict(zip(names_out, results))
    for key in fetch:
        blocks[key] = results.pop(key)
    return results


def multiply(layer, chips, work, pieces, block, named, out):
    ys = {}
    for shard in [shard for shard in pieces if any(shard in shards for shards in work.values())]:
        parts = [named["x", shard, i][...] for i in range(pieces[shard])]
        x = (parts[0] if len(parts) == 1 else jnp.concatenate(parts, 0)).astype(jnp.float32)
        if shard in work["gate"]:
            square = x * x
            q = square[:, :128]
            for lane in range(128, x.shape[1], 128):
                q = q + square[:, lane : lane + 128]
            if shard != work["gate"][0]:
                out["squares"][...] += q
            elif ("old", "squares") in named:
                out["squares"][...] = named["old", "squares"][...] + q
            else:
                out["squares"][...] = q
        ys[shard] = (x * named["gain"][layer : layer + 1, pl.ds(pl.multiple_of(shard_at(*shard, chips) * x.shape[1], x.shape[1]), x.shape[1])]).astype(jnp.bfloat16)
    for name, kind in (("up", "u"), ("gate", "g")):
        for e, shard in enumerate(work[name]):
            value = jnp.dot(ys[shard], block((kind, layer, *shard)), preferred_element_type=jnp.float32)
            if e:
                out[name][...] += value
            elif ("old", name) in named:
                out[name][...] = named["old", name][...] + value
            else:
                out[name][...] = value


def ring_body(chips, stream_in, norm_gain, w_gate, w_up, w_down):
    micro, seqs, cols = stream_in.shape
    rows = micro * seqs
    part = rows // 2
    layers, features, hid = w_gate.shape
    far = chips // 2
    ring = [chip_at(place, chips) for place in range(chips)]
    right = [(2 * ring[i] + c, 2 * ring[(i + 1) % chips] + c) for i in range(chips) for c in range(2)]
    left = [(b, a) for a, b in right]
    right2 = [(2 * ring[i] + c, 2 * ring[(i + 2) % chips] + c) for i in range(chips) for c in range(2)]
    left2 = [(b, a) for a, b in right2]
    swap = [(i, i ^ 1) for i in range(2 * chips)]
    f32, bf16 = jnp.float32, jnp.bfloat16
    weights = {"g": w_gate, "u": w_up, "d": w_down}
    blocks = {}
    kept = {}
    flops = 2 * rows * cols * hid

    def send(x, perm):
        return lax.ppermute(x, AXIS, perm)

    def fence(*groups):
        found = []

        def walk(value, visit):
            if isinstance(value, dict):
                return {key: walk(part, visit) for key, part in value.items()}
            if isinstance(value, (list, tuple)):
                return type(value)(walk(part, visit) for part in value)
            return visit(value) if isinstance(value, jax.Array) else value

        walk(groups, lambda x: found.append(x))
        kept = iter(lax.optimization_barrier(found))
        out = walk(groups, lambda x: next(kept))
        return out if len(out) > 1 else out[0]

    sums = {
        "gate": jax.ShapeDtypeStruct((rows, hid), f32),
        "up": jax.ShapeDtypeStruct((rows, hid), f32),
        "squares": jax.ShapeDtypeStruct((rows, 128), f32),
    }

    def direct(layer):
        return far == 4 and layer in DIRECT

    def both(offset):
        return [offset, -offset] if offset > 0 else [0] if offset == 0 else []

    def stages(layer):
        if direct(layer):
            return [
                [(0, False)], [(0, True), (-1, False), (1, False), (-2, False), (2, False)],
                [(-1, True), (1, True), (-2, True), (2, True), (-3, False), (3, False), (4, False)],
                [(-3, True), (3, True), (4, True)],
            ]
        shards = [[(0, False)], [(0, True), (-1, False), (1, False)]]
        shards += [[(1 - s, True), (s - 1, True), (-s, False), (s, False)] for s in range(2, far)]
        return shards + [[(1 - far, True), (far - 1, True), (far, False)], [(far, True)]]

    units = []
    for layer in range(layers):
        units += [[("g", layer, *shard), ("u", layer, *shard)] for shards in stages(layer) for shard in shards]
        units += [[("d", layer, o, True), ("d", layer, o, False)] for step in range(far, -1, -1) for o in
                  ([far] if step == far else both(step))]
    weights["units"] = units

    def ahead(layer, name):
        return AHEAD.get((layer, name), 0)

    def shards_in(layer, xs, work, acc):
        ins = {"gain": kept["gain"]} if kept else {}
        ins.update({("x", shard, i): x for shard, arrays in xs.items() for i, x in enumerate(arrays) if kept})
        ins.update({("old", name): value for name, value in acc.items()})
        keys = [(kind, layer, *s) for name, kind in (("up", "u"), ("gate", "g")) for s in work[name]]
        return ins, keys, {shard: len(arrays) for shard, arrays in xs.items()}

    def gate_up(layer, xs, acc, fetch):
        work = {"gate": list(xs), "up": list(xs)}
        ins, keys, pieces = shards_in(layer, xs, work, acc)
        outs = {name: s for name, s in sums.items() if name in acc or work.get(name, work["gate"])}

        def job(block, named, out, scratch):
            multiply(layer, chips, work, pieces, block, named, out)

        raw = {} if kept else {"gain": norm_gain, ("x", (0, False), 0): stream}
        out = stage(
            chips, weights, blocks, job, keys, ins, outs, {("old", name): name for name in acc}, [], fetch,
            len(keys) * flops, "gate_up", raw,
        )
        for name in raw:
            kept[name] = out.pop(name)
        return out

    def finish(layer, xs, acc, fetch):
        work = {"gate": list(xs), "up": list(xs)}
        ins, keys, pieces = shards_in(layer, xs, work, acc)

        def job(block, named, out, scratch):
            into = dict(zip(sums, scratch))
            multiply(layer, chips, work, pieces, block, named, into)
            meansq = jnp.sum(into["squares"][...], axis=1, keepdims=True) / features
            scale = lax.rsqrt(meansq + EPS)
            g = into["gate"][...] * scale
            hidden = (g / (1.0 + jnp.exp(-g)) * (into["up"][...] * scale)).astype(bf16)
            out["hidden"][...] = hidden
            project(layer, [far], hidden, block, out)

        outs = {"hidden": jax.ShapeDtypeStruct((rows, hid), bf16), **chunk_shapes([far])}
        scratch = [pltpu.VMEM(s.shape, s.dtype) for s in sums.values()]
        return stage(
            chips, weights, blocks, job, keys + [("d", layer, far, s) for s in (True, False)], ins, outs, {},
            scratch, fetch, (len(keys) + 2) * flops, "hidden",
        )

    def chunk_shapes(offsets):
        outs = {("sib", o): jax.ShapeDtypeStruct((rows, cols), bf16) for o in offsets}
        outs.update({("own", o): jax.ShapeDtypeStruct((rows, cols), f32) for o in offsets})
        return outs

    def project(layer, offsets, hidden, block, out):
        for o in offsets:
            sib = jnp.dot(hidden, block(("d", layer, o, True)), preferred_element_type=f32)
            out["sib", o][...] = sib.astype(bf16)
            out["own", o][...] = jnp.dot(hidden, block(("d", layer, o, False)), preferred_element_type=f32)

    def down(layer, offsets, hidden, fetch):
        def job(block, named, out, scratch):
            project(layer, offsets, named["hidden"][...], block, out)

        keys = [("d", layer, o, s) for o in offsets for s in (True, False)]
        return stage(
            chips, weights, blocks, job, keys, {"hidden": hidden}, chunk_shapes(offsets), {}, [], fetch,
            len(keys) * flops, "down",
        )

    stream = stream_in.reshape(rows, cols)
    for layer in range(layers):
        acc = {}
        held = {(0, False): (stream,)}
        crossing = {(0, True): (stream,)}
        if direct(layer):
            moved = {
                (-2, False): (send(stream, right2),), (2, False): (send(stream, left2),),
                (-1, False): (send(stream, right),), (1, False): (send(stream, left),),
            }
            crossed = {shard: tuple(send(x, swap) for x in xs) for shard, xs in crossing.items()}
            acc = gate_up(layer, held, acc, ahead(layer, "gather1"))
            acc, moved, crossed = fence(acc, moved, crossed)
            held = {**crossed, **moved}
            (r,), (l,) = moved[-2, False], moved[2, False]
            crossing = {(o, True): xs for (o, _), xs in moved.items()}
            moved = {
                (-3, False): (send(r, right),), (3, False): (send(l, left),),
                (4, False): (send(r[:part], right2), send(l[part:], left2)),
            }
            crossed = {shard: tuple(send(x, swap) for x in xs) for shard, xs in crossing.items()}
            acc = gate_up(layer, held, acc, ahead(layer, "gather2"))
            acc, moved, crossed = fence(acc, moved, crossed)
            held = {**crossed, **moved}
            crossing = {(o, True): xs for (o, _), xs in moved.items()}
        else:
            r = l = stream
            for step in range(1, far + 1):
                if step > 1:
                    r, acc, held = fence(r, acc, held)
                    l, held = fence(l, held)
                    crossing = {(1 - step, True): (r,), (step - 1, True): (l,)}
                    held = {**held, (1 - step, False): (r,), (step - 1, False): (l,)}
                if step == far:
                    r, l = r[:part], l[part:]
                r, l = send(r, right), send(l, left)
                crossed = {shard: tuple(send(x, swap) for x in xs) for shard, xs in crossing.items()}
                acc = gate_up(layer, held, acc, ahead(layer, "gather%d" % step))
                held = crossed
            r, l, acc, held = fence(r, l, acc, held)
            held = {**held, (far, False): (r, l)}
            crossing = {(far, True): (r, l)}
        crossed = {shard: tuple(send(x, swap) for x in xs) for shard, xs in crossing.items()}
        acc = gate_up(layer, held, acc, ahead(layer, "gathered"))
        acc, crossed = fence(acc, crossed)
        found = finish(layer, crossed, acc, ahead(layer, "hidden"))
        hidden, found = fence(found.pop("hidden"), found)
        c = send(found["sib", far], swap)
        own = found["own", far]
        found = down(layer, both(far - 1), hidden, ahead(layer, "scatter%d" % far))
        c, found = fence(c, found)
        total = (own + c.astype(f32)).astype(bf16)
        hidden, total = fence(hidden, total)
        r, l = total[:part], total[part:]
        for step in range(far - 1, -1, -1):
            r, l = send(r, right), send(l, left)
            if not step:
                if ahead(layer, "scatter0"):
                    count = ahead(layer, "scatter0")
                    stage(chips, weights, blocks, lambda *given: None, [], {"hidden": hidden}, {}, {}, [], count, 0, "ahead")
                break
            c = [send(found["sib", o], swap) for o in both(step)]
            own = [found["own", o] for o in both(step)]
            found = down(layer, both(step - 1), hidden, ahead(layer, "scatter%d" % step))
            if step == far - 1:
                hole = jnp.zeros((part, cols), bf16)
                r, l = jnp.concatenate([r, hole], 0), jnp.concatenate([hole, l], 0)
            l, c, found = fence(l, c, found)
            l = fence((own[1] + c[1].astype(f32) + l.astype(f32)).astype(bf16))
            r, _ = fence(r, l)
            r = (own[0] + c[0].astype(f32) + r.astype(f32)).astype(bf16)
            hidden, r = fence(hidden, r)
            if step == 1:
                c = send(found["sib", 0], swap)
        r, l, c, _ = fence(r, l, c, dict(blocks))
        branch = found["own", 0] + c.astype(f32) + r.astype(f32) + l.astype(f32)
        stream = (stream.astype(f32) + branch).astype(bf16)
    return stream.reshape(micro, seqs, cols)


def plain_body(stream_in, norm_gain, w_gate, w_up, w_down):
    micro, seqs, cols = stream_in.shape
    layers = w_gate.shape[0]
    f32, bf16 = jnp.float32, jnp.bfloat16
    stream = stream_in.reshape(micro * seqs, cols)
    for layer in range(layers):
        whole = lax.all_gather(stream, AXIS, axis=1, tiled=True).astype(f32)
        meansq = jnp.mean(whole * whole, axis=1, keepdims=True)
        normed = (whole * lax.rsqrt(meansq + EPS) * norm_gain[layer]).astype(bf16)
        gate_out = jnp.dot(normed, w_gate[layer], preferred_element_type=f32)
        up_out = jnp.dot(normed, w_up[layer], preferred_element_type=f32)
        hidden = (jax.nn.silu(gate_out) * up_out).astype(bf16)
        partials = jnp.dot(hidden, w_down[layer], preferred_element_type=f32)
        branch = lax.psum_scatter(partials, AXIS, scatter_dimension=1, tiled=True)
        stream = (stream.astype(f32) + branch).astype(bf16)
    return stream.reshape(micro, seqs, cols)


def solution(mesh):
    devices = mesh.shape[AXIS]

    def body(stream_in, *rest):
        cols = stream_in.shape[2]
        if devices % 8 == 0 and cols % 128 == 0:
            return ring_body(devices // 2, stream_in, *rest)
        return plain_body(stream_in, *rest)

    return jax.shard_map(
        body,
        mesh=mesh,
        in_specs=(
            P(None, "groups", AXIS),
            P(),
            P(None, None, AXIS),
            P(None, None, AXIS),
            P(None, AXIS, None),
        ),
        out_specs=P(None, "groups", AXIS),
        check_vma=False,
    )
```

```python
import functools

import jax
import jax.numpy as jnp
from jax import lax
from jax.experimental import pallas as pl
from jax.experimental.pallas import tpu as pltpu
from jax.sharding import PartitionSpec as P

AXIS = "width"
EPS = 1e-05
VMEM = pl.BlockSpec(memory_space=pltpu.VMEM)
HBM = pl.BlockSpec(memory_space=pl.ANY)
LIMIT = 20 * 1024 * 1024
AHEAD = {
    (0, "gather1"): 4, (0, "gather2"): 4, (0, "gather3"): 4, (0, "gather4"): 3, (0, "gathered"): 0, (0, "last"): 3,
    (0, "scatter2"): 2, (0, "scatter1"): 4, (0, "scatter0"): 7,
    (1, "gather1"): 3, (1, "gather2"): 1, (1, "gather3"): 1, (1, "gather4"): 2,
}


def place_of(chip, chips):
    half = chip // 2
    return half + (chip - 2 * half) * (chips - 1 - 2 * half)


def chip_at(place, chips):
    far = (place >= chips // 2) * 1
    return 2 * place + far * (2 * chips - 1 - 4 * place)


def shard_at(offset, sibling, chips):
    me = lax.axis_index(AXIS)
    chip = me // 2
    core = me - 2 * chip
    place = lax.rem(place_of(chip, chips) + (offset + chips), chips)
    far = jnp.where(place >= chips // 2, 1, 0)
    there = 2 * place + far * (2 * chips - 1 - 4 * place)
    return 2 * there + (1 - core if sibling else core)


def view(key, ref, chips):
    kind, layer, offset, sibling = key
    size = ref.shape[2 if kind == "d" else 1] // (2 * chips)
    span = pl.ds(pl.multiple_of(shard_at(offset, sibling, chips) * size, size), size)
    return ref.at[layer, :, span] if kind == "d" else ref.at[layer, span, :]


def stage_kernel(chips, job, raw, stream, fetch, names_in, names_out, *refs):
    named = dict(zip(names_in, refs))
    out = dict(zip(names_out, refs[len(names_in) :]))
    scratch = list(refs[len(names_in) + len(names_out) :])
    copies = {}
    if raw or stream or fetch:
        sems = scratch.pop()
        for e, name in enumerate(raw):
            copies[name] = pltpu.make_async_copy(named["raw", name], out[name], sems.at[len(stream + fetch) + e])
            copies[name].start()
            named[name] = out[name]
        for e, key in enumerate(stream + fetch):
            if key in stream:
                named[key] = scratch.pop(0)
            to = named[key] if key in stream else out[key]
            copies[key] = pltpu.make_async_copy(view(key, named["hbm", key[0]], chips), to, sems.at[e])
            copies[key].start()

    def block(key):
        if key in copies:
            copies[key].wait()
        return named[key][...]

    for name in raw:
        copies[name].wait()
    job(block, named, out, scratch)
    for key in fetch:
        copies[key].wait()


def stage(chips, weights, blocks, job, keys, inputs, outputs, aliases, scratch, ahead, flops, name, raw=()):
    ins = dict(inputs)
    stream = []
    units = [unit for unit in weights["units"] if unit[0] not in keys]
    fetch = [key for unit in units[:ahead] for key in unit]
    weights["units"] = units[ahead:]
    for key in keys:
        if key in blocks:
            ins[key] = blocks.pop(key)
        else:
            stream.append(key)
    _, features, hid = weights["g"].shape
    size = features // (2 * chips)
    shapes = {key: (hid, size) if key[0] == "d" else (size, hid) for key in stream + fetch}
    kinds = sorted({key[0] for key in stream + fetch})
    names_in = list(ins) + [("hbm", kind) for kind in kinds] + [("raw", key) for key in raw]
    out_shape = dict(outputs)
    for key in raw:
        out_shape[key] = jax.ShapeDtypeStruct(raw[key].shape, raw[key].dtype)
    for key in fetch:
        out_shape[key] = jax.ShapeDtypeStruct(shapes[key], jnp.bfloat16)
    names_out = list(out_shape)
    scratch = [pltpu.VMEM(shapes[key], jnp.bfloat16) for key in stream] + scratch
    if raw or stream or fetch:
        scratch.append(pltpu.SemaphoreType.DMA((len(stream + fetch) + len(raw),)))
    results = pl.pallas_call(
        functools.partial(stage_kernel, chips, job, list(raw), stream, fetch, names_in, names_out),
        out_shape=list(out_shape.values()),
        in_specs=[VMEM] * len(ins) + [HBM] * (len(kinds) + len(raw)),
        out_specs=[VMEM] * len(names_out),
        scratch_shapes=scratch,
        input_output_aliases={names_in.index(a): names_out.index(b) for a, b in aliases.items()},
        compiler_params=pltpu.CompilerParams(vmem_limit_bytes=LIMIT),
        cost_estimate=pl.CostEstimate(
            flops=flops, bytes_accessed=sum(2 * a * b for a, b in shapes.values()), transcendentals=0
        ),
        name=name,
    )(
        *ins.values(),
        *(pltpu.with_memory_space_constraint(x, pltpu.HBM) for x in [*(weights[k] for k in kinds), *dict(raw).values()]),
    )
    results = dict(zip(names_out, results))
    for key in fetch:
        blocks[key] = results.pop(key)
    return results


def multiply(layer, chips, shards, block, named, out):
    def add(name, value, e):
        if e:
            out[name][...] += value
        elif ("old", name) in named:
            out[name][...] = named["old", name][...] + value
        else:
            out[name][...] = value

    ys = {}
    for e, shard in enumerate(shards):
        x = named["x", shard][...].astype(jnp.float32)
        size = x.shape[1]
        square = x * x
        add("squares", sum(square[:, lane : lane + 128] for lane in range(0, size, 128)), e)
        span = pl.ds(pl.multiple_of(shard_at(*shard, chips) * size, size), size)
        ys[shard] = (x * named["gain"][layer : layer + 1, span]).astype(jnp.bfloat16)
    for name, kind in (("up", "u"), ("gate", "g")):
        for e, shard in enumerate(shards):
            add(name, jnp.dot(ys[shard], block((kind, layer, *shard)), preferred_element_type=jnp.float32), e)


def ring_body(chips, stream_in, norm_gain, w_gate, w_up, w_down):
    micro, seqs, cols = stream_in.shape
    rows = micro * seqs
    layers, features, hid = w_gate.shape
    far = chips // 2
    ring = [chip_at(place, chips) for place in range(chips)]
    right = [(2 * ring[i] + c, 2 * ring[(i + 1) % chips] + c) for i in range(chips) for c in range(2)]
    left = [(b, a) for a, b in right]
    swap = [(i, i ^ 1) for i in range(2 * chips)]
    f32, bf16 = jnp.float32, jnp.bfloat16
    weights = {"g": w_gate, "u": w_up, "d": w_down}
    blocks = {}
    kept = {}
    flops = 2 * rows * cols * hid

    def send(x, perm):
        return lax.ppermute(x, AXIS, perm)

    def fence(*groups):
        found = []

        def walk(value, visit):
            if isinstance(value, dict):
                return {key: walk(part, visit) for key, part in value.items()}
            if isinstance(value, (list, tuple)):
                return type(value)(walk(part, visit) for part in value)
            return visit(value) if isinstance(value, jax.Array) else value

        walk(groups, lambda x: found.append(x))
        kept = iter(lax.optimization_barrier(found))
        out = walk(groups, lambda x: next(kept))
        return out if len(out) > 1 else out[0]

    sums = {
        "gate": jax.ShapeDtypeStruct((rows, hid), f32),
        "up": jax.ShapeDtypeStruct((rows, hid), f32),
        "squares": jax.ShapeDtypeStruct((rows, 128), f32),
    }

    def both(offset):
        return [offset, -offset] if offset > 0 else [0] if offset == 0 else []

    stages = [[(0, False)], [(0, True), (-1, False), (1, False)]]
    stages += [[(1 - s, True), (s - 1, True), (-s, False), (s, False)] for s in range(2, far)]
    stages += [[(1 - far, True)], [(far - 1, True), (far, False)], [(far, True)]]

    units = []
    for layer in range(layers):
        units += [[("g", layer, *shard), ("u", layer, *shard)] for shards in stages for shard in shards]
        units += [[("d", layer, o, True), ("d", layer, o, False)] for step in range(far, -1, -1) for o in
                  ([far] if step == far else both(step))]
    weights["units"] = units

    def ahead(layer, name):
        return AHEAD.get((layer, name), 0)

    def shards_in(layer, xs, acc):
        ins = {"gain": kept["gain"]} if kept else {}
        ins.update({("x", shard): x for shard, x in xs.items() if kept})
        ins.update({("old", name): value for name, value in acc.items()})
        keys = [(kind, layer, *shard) for kind in "ug" for shard in xs]
        return ins, keys

    def gate_up(layer, xs, acc, fetch):
        ins, keys = shards_in(layer, xs, acc)
        outs = sums

        def job(block, named, out, scratch):
            multiply(layer, chips, list(xs), block, named, out)

        raw = {} if kept else {"gain": norm_gain, ("x", (0, False)): stream}
        out = stage(
            chips, weights, blocks, job, keys, ins, outs, {("old", name): name for name in acc}, [], fetch,
            len(keys) * flops, "gate_up", raw,
        )
        for name in raw:
            kept[name] = out.pop(name)
        return out

    def finish(layer, xs, acc, fetch):
        ins, keys = shards_in(layer, xs, acc)

        def job(block, named, out, scratch):
            into = dict(zip(sums, scratch))
            multiply(layer, chips, list(xs), block, named, into)
            meansq = jnp.sum(into["squares"][...], axis=1, keepdims=True) / features
            scale = lax.rsqrt(meansq + EPS)
            g = into["gate"][...] * scale
            hidden = (g / (1.0 + jnp.exp(-g)) * (into["up"][...] * scale)).astype(bf16)
            out["hidden"][...] = hidden
            project(layer, [far], hidden, block, out)

        outs = {"hidden": jax.ShapeDtypeStruct((rows, hid), bf16), **chunk_shapes([far])}
        scratch = [pltpu.VMEM(s.shape, s.dtype) for s in sums.values()]
        return stage(
            chips, weights, blocks, job, keys + [("d", layer, far, s) for s in (True, False)], ins, outs, {},
            scratch, fetch, (len(keys) + 2) * flops, "hidden",
        )

    def chunk_shapes(offsets):
        outs = {("sib", o): jax.ShapeDtypeStruct((rows, cols), bf16) for o in offsets}
        outs.update({("own", o): jax.ShapeDtypeStruct((rows, cols), f32) for o in offsets})
        return outs

    def project(layer, offsets, hidden, block, out):
        for o in offsets:
            sib = jnp.dot(hidden, block(("d", layer, o, True)), preferred_element_type=f32)
            out["sib", o][...] = sib.astype(bf16)
            out["own", o][...] = jnp.dot(hidden, block(("d", layer, o, False)), preferred_element_type=f32)

    def down(layer, offsets, hidden, fetch):
        def job(block, named, out, scratch):
            project(layer, offsets, named["hidden"][...], block, out)

        keys = [("d", layer, o, s) for o in offsets for s in (True, False)]
        return stage(
            chips, weights, blocks, job, keys, {"hidden": hidden}, chunk_shapes(offsets), {}, [], fetch,
            len(keys) * flops, "down",
        )

    stream = stream_in.reshape(rows, cols)
    for layer in range(layers):
        r = l = stream
        acc = {}
        held = {(0, False): stream}
        crossed = {(0, True): send(stream, swap)}
        for step in range(1, far + 1):
            r = send(r, right)
            if step < far:
                l = send(l, left)
            acc = gate_up(layer, held, acc, ahead(layer, "gather%d" % step))
            if step == far:
                l, acc, crossed = fence(l, acc, crossed)
                late = send(l, swap)
                acc = gate_up(layer, {(far - 1, False): l, **crossed}, acc, ahead(layer, "gathered"))
                r, late, acc = fence(r, late, acc)
                break
            r, acc = fence(r, acc)
            held = {**crossed, (-step, False): r}
            crossed = {(-step, True): send(r, swap)}
            if step + 1 < far:
                l, held = fence(l, held)
                held[step, False] = l
                crossed[step, True] = send(l, swap)
        crossed = {(far, True): send(r, swap)}
        acc = gate_up(layer, {(far - 1, True): late, (far, False): r}, acc, ahead(layer, "last"))
        acc, crossed = fence(acc, crossed)
        found = finish(layer, crossed, acc, ahead(layer, "hidden"))
        hidden, found = fence(found.pop("hidden"), found)
        c = send(found["sib", far], swap)
        own = found["own", far]
        found = down(layer, both(far - 1), hidden, ahead(layer, "scatter%d" % far))
        c, found = fence(c, found)
        total = (own + c.astype(f32)).astype(bf16)
        hidden, total = fence(hidden, total)
        r, l = total[: rows // 2], total[rows // 2 :]
        for step in range(far - 1, -1, -1):
            r, l = send(r, right), send(l, left)
            if not step:
                if ahead(layer, "scatter0"):
                    count = ahead(layer, "scatter0")
                    stage(chips, weights, blocks, lambda *given: None, [], {"hidden": hidden}, {}, {}, [], count, 0, "ahead")
                break
            c = [send(found["sib", o], swap) for o in both(step)]
            own = [found["own", o] for o in both(step)]
            found = down(layer, both(step - 1), hidden, ahead(layer, "scatter%d" % step))
            l, c, found = fence(l, c, found)
            if step == far - 1:
                l = jnp.concatenate([jnp.zeros_like(l), l], 0)
            l = fence((own[1] + c[1].astype(f32) + l.astype(f32)).astype(bf16))
            r, _ = fence(r, l)
            if step == far - 1:
                r = jnp.concatenate([r, jnp.zeros_like(r)], 0)
            r = (own[0] + c[0].astype(f32) + r.astype(f32)).astype(bf16)
            hidden, r = fence(hidden, r)
            if step == 1:
                c = send(found["sib", 0], swap)
        r, l, c, _ = fence(r, l, c, dict(blocks))
        branch = found["own", 0] + c.astype(f32) + r.astype(f32) + l.astype(f32)
        stream = (stream.astype(f32) + branch).astype(bf16)
    return stream.reshape(micro, seqs, cols)


def plain_body(stream_in, norm_gain, w_gate, w_up, w_down):
    micro, seqs, cols = stream_in.shape
    layers = w_gate.shape[0]
    f32, bf16 = jnp.float32, jnp.bfloat16
    stream = stream_in.reshape(micro * seqs, cols)
    for layer in range(layers):
        whole = lax.all_gather(stream, AXIS, axis=1, tiled=True).astype(f32)
        meansq = jnp.mean(whole * whole, axis=1, keepdims=True)
        normed = (whole * lax.rsqrt(meansq + EPS) * norm_gain[layer]).astype(bf16)
        gate_out = jnp.dot(normed, w_gate[layer], preferred_element_type=f32)
        up_out = jnp.dot(normed, w_up[layer], preferred_element_type=f32)
        hidden = (jax.nn.silu(gate_out) * up_out).astype(bf16)
        partials = jnp.dot(hidden, w_down[layer], preferred_element_type=f32)
        branch = lax.psum_scatter(partials, AXIS, scatter_dimension=1, tiled=True)
        stream = (stream.astype(f32) + branch).astype(bf16)
    return stream.reshape(micro, seqs, cols)


def solution(mesh):
    devices = mesh.shape[AXIS]

    def body(stream_in, *rest):
        cols = stream_in.shape[2]
        if devices >= 16 and devices % 4 == 0 and cols % 128 == 0:
            return ring_body(devices // 2, stream_in, *rest)
        return plain_body(stream_in, *rest)

    return jax.shard_map(
        body,
        mesh=mesh,
        in_specs=(
            P(None, "groups", AXIS),
            P(),
            P(None, None, AXIS),
            P(None, None, AXIS),
            P(None, AXIS, None),
        ),
        out_specs=P(None, "groups", AXIS),
        check_vma=False,
    )
```

```python
import functools

import jax
import jax.numpy as jnp
from jax import lax
from jax.experimental import pallas as pl
from jax.experimental.pallas import tpu as pltpu
from jax.sharding import PartitionSpec as P

AXIS = "width"
EPS = 1e-05
VMEM = pl.BlockSpec(memory_space=pltpu.VMEM)
HBM = pl.BlockSpec(memory_space=pl.ANY)
LIMIT = 20 * 1024 * 1024
AHEAD = {
    (0, "gather1"): 4, (0, "gather2"): 4, (0, "gather3"): 4, (0, "gather4"): 3, (0, "gathered"): 0, (0, "last"): 3,
    (0, "scatter2"): 2, (0, "scatter1"): 4, (0, "scatter0"): 6,
    (1, "gather1"): 4, (1, "gather2"): 2, (1, "gather4"): 2,
}


def place_of(chip, chips):
    half = chip // 2
    return half + (chip - 2 * half) * (chips - 1 - 2 * half)


def chip_at(place, chips):
    far = (place >= chips // 2) * 1
    return 2 * place + far * (2 * chips - 1 - 4 * place)


def shard_at(offset, sibling, chips):
    me = lax.axis_index(AXIS)
    chip = me // 2
    core = me - 2 * chip
    place = lax.rem(place_of(chip, chips) + (offset + chips), chips)
    far = jnp.where(place >= chips // 2, 1, 0)
    there = 2 * place + far * (2 * chips - 1 - 4 * place)
    return 2 * there + (1 - core if sibling else core)


def view(key, ref, chips):
    kind, layer, offset, sibling = key
    size = ref.shape[2 if kind == "d" else 1] // (2 * chips)
    span = pl.ds(pl.multiple_of(shard_at(offset, sibling, chips) * size, size), size)
    return ref.at[layer, :, span] if kind == "d" else ref.at[layer, span, :]


def stage_kernel(chips, job, raw, stream, fetch, names_in, names_out, *refs):
    named = dict(zip(names_in, refs))
    out = dict(zip(names_out, refs[len(names_in) :]))
    scratch = list(refs[len(names_in) + len(names_out) :])
    copies = {}
    if raw or stream or fetch:
        sems = scratch.pop()
        for e, name in enumerate(raw):
            copies[name] = pltpu.make_async_copy(named["raw", name], out[name], sems.at[len(stream + fetch) + e])
            copies[name].start()
            named[name] = out[name]
        for e, key in enumerate(stream + fetch):
            if key in stream:
                named[key] = scratch.pop(0)
            to = named[key] if key in stream else out[key]
            copies[key] = pltpu.make_async_copy(view(key, named["hbm", key[0]], chips), to, sems.at[e])
            copies[key].start()

    def block(key):
        if key in copies:
            copies[key].wait()
        return named[key][...]

    for name in raw:
        copies[name].wait()
    job(block, named, out, scratch)
    for key in fetch:
        copies[key].wait()


def stage(chips, weights, blocks, job, keys, inputs, outputs, aliases, scratch, ahead, flops, name, raw=()):
    ins = dict(inputs)
    stream = []
    units = [unit for unit in weights["units"] if unit[0] not in keys]
    fetch = [key for unit in units[:ahead] for key in unit]
    weights["units"] = units[ahead:]
    for key in keys:
        if key in blocks:
            ins[key] = blocks.pop(key)
        else:
            stream.append(key)
    _, features, hid = weights["g"].shape
    size = features // (2 * chips)
    shapes = {key: (hid, size) if key[0] == "d" else (size, hid) for key in stream + fetch}
    kinds = sorted({key[0] for key in stream + fetch})
    names_in = list(ins) + [("hbm", kind) for kind in kinds] + [("raw", key) for key in raw]
    out_shape = dict(outputs)
    for key in raw:
        out_shape[key] = jax.ShapeDtypeStruct(raw[key].shape, raw[key].dtype)
    for key in fetch:
        out_shape[key] = jax.ShapeDtypeStruct(shapes[key], jnp.bfloat16)
    names_out = list(out_shape)
    scratch = [pltpu.VMEM(shapes[key], jnp.bfloat16) for key in stream] + scratch
    if raw or stream or fetch:
        scratch.append(pltpu.SemaphoreType.DMA((len(stream + fetch) + len(raw),)))
    results = pl.pallas_call(
        functools.partial(stage_kernel, chips, job, list(raw), stream, fetch, names_in, names_out),
        out_shape=list(out_shape.values()),
        in_specs=[VMEM] * len(ins) + [HBM] * (len(kinds) + len(raw)),
        out_specs=[VMEM] * len(names_out),
        scratch_shapes=scratch,
        input_output_aliases={names_in.index(a): names_out.index(b) for a, b in aliases.items()},
        compiler_params=pltpu.CompilerParams(vmem_limit_bytes=LIMIT),
        cost_estimate=pl.CostEstimate(
            flops=flops, bytes_accessed=sum(2 * a * b for a, b in shapes.values()), transcendentals=0
        ),
        name=name,
    )(
        *ins.values(),
        *(pltpu.with_memory_space_constraint(x, pltpu.HBM) for x in [*(weights[k] for k in kinds), *dict(raw).values()]),
    )
    results = dict(zip(names_out, results))
    for key in fetch:
        blocks[key] = results.pop(key)
    return results


def multiply(layer, chips, shards, block, named, out):
    def add(name, value, e):
        if e:
            out[name][...] += value
        elif ("old", name) in named:
            out[name][...] = named["old", name][...] + value
        else:
            out[name][...] = value

    ys = {}
    for e, shard in enumerate(shards):
        x = named["x", shard][...].astype(jnp.float32)
        size = x.shape[1]
        square = x * x
        add("squares", sum(square[:, lane : lane + 128] for lane in range(0, size, 128)), e)
        span = pl.ds(pl.multiple_of(shard_at(*shard, chips) * size, size), size)
        ys[shard] = (x * named["gain"][layer : layer + 1, span]).astype(jnp.bfloat16)
    for name, kind in (("up", "u"), ("gate", "g")):
        for e, shard in enumerate(shards):
            add(name, jnp.dot(ys[shard], block((kind, layer, *shard)), preferred_element_type=jnp.float32), e)


def ring_body(chips, stream_in, norm_gain, w_gate, w_up, w_down):
    micro, seqs, cols = stream_in.shape
    rows = micro * seqs
    layers, features, hid = w_gate.shape
    far = chips // 2
    ring = [chip_at(place, chips) for place in range(chips)]
    right = [(2 * ring[i] + c, 2 * ring[(i + 1) % chips] + c) for i in range(chips) for c in range(2)]
    left = [(b, a) for a, b in right]
    swap = [(i, i ^ 1) for i in range(2 * chips)]
    f32, bf16 = jnp.float32, jnp.bfloat16
    weights = {"g": w_gate, "u": w_up, "d": w_down}
    blocks = {}
    kept = {}
    flops = 2 * rows * cols * hid

    def send(x, perm):
        return lax.ppermute(x, AXIS, perm)

    def fence(*groups):
        found = []

        def walk(value, visit):
            if isinstance(value, dict):
                return {key: walk(part, visit) for key, part in value.items()}
            if isinstance(value, (list, tuple)):
                return type(value)(walk(part, visit) for part in value)
            return visit(value) if isinstance(value, jax.Array) else value

        walk(groups, lambda x: found.append(x))
        kept = iter(lax.optimization_barrier(found))
        out = walk(groups, lambda x: next(kept))
        return out if len(out) > 1 else out[0]

    sums = {
        "gate": jax.ShapeDtypeStruct((rows, hid), f32),
        "up": jax.ShapeDtypeStruct((rows, hid), f32),
        "squares": jax.ShapeDtypeStruct((rows, 128), f32),
    }

    def both(offset):
        return [offset, -offset] if offset > 0 else [0] if offset == 0 else []

    stages = [[(0, False)], [(0, True), (-1, False), (1, False)]]
    stages += [[(1 - s, True), (s - 1, True), (-s, False), (s, False)] for s in range(2, far)]
    stages += [[(1 - far, True)], [(far - 1, True), (far, False)], [(far, True)]]

    units = []
    for layer in range(layers):
        units += [[("g", layer, *shard), ("u", layer, *shard)] for shards in stages for shard in shards]
        units += [[("d", layer, o, True), ("d", layer, o, False)] for step in range(far, -1, -1) for o in
                  ([far] if step == far else both(step))]
    weights["units"] = units

    def ahead(layer, name):
        return AHEAD.get((layer, name), 0)

    def shards_in(layer, xs, acc):
        ins = {"gain": kept["gain"]} if kept else {}
        ins.update({("x", shard): x for shard, x in xs.items() if kept})
        ins.update({("old", name): value for name, value in acc.items()})
        keys = [(kind, layer, *shard) for kind in "ug" for shard in xs]
        return ins, keys

    def gate_up(layer, xs, acc, fetch):
        ins, keys = shards_in(layer, xs, acc)
        outs = sums

        def job(block, named, out, scratch):
            multiply(layer, chips, list(xs), block, named, out)

        raw = {} if kept else {"gain": norm_gain, ("x", (0, False)): stream}
        out = stage(
            chips, weights, blocks, job, keys, ins, outs, {("old", name): name for name in acc}, [], fetch,
            len(keys) * flops, "gate_up", raw,
        )
        for name in raw:
            kept[name] = out.pop(name)
        return out

    def finish(layer, xs, acc, fetch):
        ins, keys = shards_in(layer, xs, acc)

        def job(block, named, out, scratch):
            into = dict(zip(sums, scratch))
            multiply(layer, chips, list(xs), block, named, into)
            meansq = jnp.sum(into["squares"][...], axis=1, keepdims=True) / features
            scale = lax.rsqrt(meansq + EPS)
            g = into["gate"][...] * scale
            hidden = (g / (1.0 + jnp.exp(-g)) * (into["up"][...] * scale)).astype(bf16)
            out["hidden"][...] = hidden
            project(layer, [far], hidden, block, out)

        outs = {"hidden": jax.ShapeDtypeStruct((rows, hid), bf16), **chunk_shapes([far])}
        scratch = [pltpu.VMEM(s.shape, s.dtype) for s in sums.values()]
        return stage(
            chips, weights, blocks, job, keys + [("d", layer, far, s) for s in (True, False)], ins, outs, {},
            scratch, fetch, (len(keys) + 2) * flops, "hidden",
        )

    def chunk_shapes(offsets):
        outs = {("sib", o): jax.ShapeDtypeStruct((rows, cols), bf16) for o in offsets}
        outs.update({("own", o): jax.ShapeDtypeStruct((rows, cols), f32) for o in offsets})
        return outs

    def project(layer, offsets, hidden, block, out):
        for o in offsets:
            sib = jnp.dot(hidden, block(("d", layer, o, True)), preferred_element_type=f32)
            out["sib", o][...] = sib.astype(bf16)
            out["own", o][...] = jnp.dot(hidden, block(("d", layer, o, False)), preferred_element_type=f32)

    def down(layer, offsets, hidden, fetch):
        def job(block, named, out, scratch):
            project(layer, offsets, named["hidden"][...], block, out)

        keys = [("d", layer, o, s) for o in offsets for s in (True, False)]
        return stage(
            chips, weights, blocks, job, keys, {"hidden": hidden}, chunk_shapes(offsets), {}, [], fetch,
            len(keys) * flops, "down",
        )

    stream = stream_in.reshape(rows, cols)
    for layer in range(layers):
        r = l = stream
        acc = {}
        held = {(0, False): stream}
        crossed = {(0, True): send(stream, swap)}
        for step in range(1, far + 1):
            r = send(r, right)
            if step < far:
                l = send(l, left)
            acc = gate_up(layer, held, acc, ahead(layer, "gather%d" % step))
            if step == far:
                l, acc, crossed = fence(l, acc, crossed)
                late = send(l, swap)
                acc = gate_up(layer, {(far - 1, False): l, **crossed}, acc, ahead(layer, "gathered"))
                r, late, acc = fence(r, late, acc)
                break
            r, acc = fence(r, acc)
            held = {**crossed, (-step, False): r}
            crossed = {(-step, True): send(r, swap)}
            if step + 1 < far:
                l, held = fence(l, held)
                held[step, False] = l
                crossed[step, True] = send(l, swap)
        crossed = {(far, True): send(r, swap)}
        acc = gate_up(layer, {(far - 1, True): late, (far, False): r}, acc, ahead(layer, "last"))
        acc, crossed = fence(acc, crossed)
        found = finish(layer, crossed, acc, ahead(layer, "hidden"))
        hidden, found = fence(found.pop("hidden"), found)
        c = send(found["sib", far], swap)
        own = found["own", far]
        found = down(layer, both(far - 1), hidden, ahead(layer, "scatter%d" % far))
        c, found = fence(c, found)
        total = (own + c.astype(f32)).astype(bf16)
        hidden, total = fence(hidden, total)
        r, l = total[: rows // 2], total[rows // 2 :]
        for step in range(far - 1, -1, -1):
            r, l = send(r, right), send(l, left)
            if not step:
                if ahead(layer, "scatter0"):
                    count = ahead(layer, "scatter0")
                    stage(chips, weights, blocks, lambda *given: None, [], {"hidden": hidden}, {}, {}, [], count, 0, "ahead")
                break
            c = [send(found["sib", o], swap) for o in both(step)]
            own = [found["own", o] for o in both(step)]
            found = down(layer, both(step - 1), hidden, ahead(layer, "scatter%d" % step))
            l, c, found = fence(l, c, found)
            if step == far - 1:
                l = jnp.concatenate([jnp.zeros_like(l), l], 0)
            l = fence((own[1] + c[1].astype(f32) + l.astype(f32)).astype(bf16))
            r, _ = fence(r, l)
            if step == far - 1:
                r = jnp.concatenate([r, jnp.zeros_like(r)], 0)
            r = (own[0] + c[0].astype(f32) + r.astype(f32)).astype(bf16)
            hidden, r = fence(hidden, r)
            if step == 1:
                c = send(found["sib", 0], swap)
        r, l, c, _ = fence(r, l, c, dict(blocks))
        branch = found["own", 0] + c.astype(f32) + r.astype(f32) + l.astype(f32)
        stream = (stream.astype(f32) + branch).astype(bf16)
    return stream.reshape(micro, seqs, cols)


def plain_body(stream_in, norm_gain, w_gate, w_up, w_down):
    micro, seqs, cols = stream_in.shape
    layers = w_gate.shape[0]
    f32, bf16 = jnp.float32, jnp.bfloat16
    stream = stream_in.reshape(micro * seqs, cols)
    for layer in range(layers):
        whole = lax.all_gather(stream, AXIS, axis=1, tiled=True).astype(f32)
        meansq = jnp.mean(whole * whole, axis=1, keepdims=True)
        normed = (whole * lax.rsqrt(meansq + EPS) * norm_gain[layer]).astype(bf16)
        gate_out = jnp.dot(normed, w_gate[layer], preferred_element_type=f32)
        up_out = jnp.dot(normed, w_up[layer], preferred_element_type=f32)
        hidden = (jax.nn.silu(gate_out) * up_out).astype(bf16)
        partials = jnp.dot(hidden, w_down[layer], preferred_element_type=f32)
        branch = lax.psum_scatter(partials, AXIS, scatter_dimension=1, tiled=True)
        stream = (stream.astype(f32) + branch).astype(bf16)
    return stream.reshape(micro, seqs, cols)


def solution(mesh):
    devices = mesh.shape[AXIS]

    def body(stream_in, *rest):
        cols = stream_in.shape[2]
        if devices >= 16 and devices % 4 == 0 and cols % 128 == 0:
            return ring_body(devices // 2, stream_in, *rest)
        return plain_body(stream_in, *rest)

    return jax.shard_map(
        body,
        mesh=mesh,
        in_specs=(
            P(None, "groups", AXIS),
            P(),
            P(None, None, AXIS),
            P(None, None, AXIS),
            P(None, AXIS, None),
        ),
        out_specs=P(None, "groups", AXIS),
        check_vma=False,
    )
```

```python
import functools

import jax
import jax.numpy as jnp
from jax import lax
from jax.experimental import pallas as pl
from jax.experimental.pallas import tpu as pltpu
from jax.sharding import PartitionSpec as P

AXIS = "width"
EPS = 1e-05
VMEM = pl.BlockSpec(memory_space=pltpu.VMEM)
HBM = pl.BlockSpec(memory_space=pl.ANY)
LIMIT = 20 * 1024 * 1024
AHEAD = {
    (0, "gather1"): 4, (0, "gather2"): 4, (0, "gather3"): 4, (0, "gather4"): 3, (0, "gathered"): 0, (0, "last"): 3,
    (0, "scatter2"): 2, (0, "scatter1"): 4, (0, "scatter0"): 6,
    (1, "gather1"): 4, (1, "gather2"): 2, (1, "gather4"): 2,
}


def place_of(chip, chips):
    half = chip // 2
    return half + (chip - 2 * half) * (chips - 1 - 2 * half)


def chip_at(place, chips):
    far = (place >= chips // 2) * 1
    return 2 * place + far * (2 * chips - 1 - 4 * place)


def shard_at(offset, sibling, chips):
    me = lax.axis_index(AXIS)
    chip = me // 2
    core = me - 2 * chip
    place = lax.rem(place_of(chip, chips) + (offset + chips), chips)
    far = jnp.where(place >= chips // 2, 1, 0)
    there = 2 * place + far * (2 * chips - 1 - 4 * place)
    return 2 * there + (1 - core if sibling else core)


def view(key, ref, chips):
    kind, layer, offset, sibling = key
    size = ref.shape[2 if kind == "d" else 1] // (2 * chips)
    span = pl.ds(pl.multiple_of(shard_at(offset, sibling, chips) * size, size), size)
    return ref.at[layer, :, span] if kind == "d" else ref.at[layer, span, :]


def stage_kernel(chips, job, raw, stream, fetch, names_in, names_out, *refs):
    named = dict(zip(names_in, refs))
    out = dict(zip(names_out, refs[len(names_in) :]))
    scratch = list(refs[len(names_in) + len(names_out) :])
    copies = {}
    if raw or stream or fetch:
        sems = scratch.pop()
        for e, name in enumerate(raw):
            copies[name] = pltpu.make_async_copy(named["raw", name], out[name], sems.at[len(stream + fetch) + e])
            copies[name].start()
            named[name] = out[name]
        for e, key in enumerate(stream + fetch):
            if key in stream:
                named[key] = scratch.pop(0)
            to = named[key] if key in stream else out[key]
            copies[key] = pltpu.make_async_copy(view(key, named["hbm", key[0]], chips), to, sems.at[e])
            copies[key].start()

    def block(key):
        if key in copies:
            copies[key].wait()
        return named[key][...]

    for name in raw:
        copies[name].wait()
    job(block, named, out, scratch)
    for key in fetch:
        copies[key].wait()


def stage(chips, weights, blocks, job, keys, inputs, outputs, aliases, scratch, ahead, flops, name, raw=()):
    ins = dict(inputs)
    stream = []
    units = [unit for unit in weights["units"] if unit[0] not in keys]
    fetch = [key for unit in units[:ahead] for key in unit]
    weights["units"] = units[ahead:]
    for key in keys:
        if key in blocks:
            ins[key] = blocks.pop(key)
        else:
            stream.append(key)
    _, features, hid = weights["g"].shape
    size = features // (2 * chips)
    shapes = {key: (hid, size) if key[0] == "d" else (size, hid) for key in stream + fetch}
    kinds = sorted({key[0] for key in stream + fetch})
    names_in = list(ins) + [("hbm", kind) for kind in kinds] + [("raw", key) for key in raw]
    out_shape = dict(outputs)
    for key in raw:
        out_shape[key] = jax.ShapeDtypeStruct(raw[key].shape, raw[key].dtype)
    for key in fetch:
        out_shape[key] = jax.ShapeDtypeStruct(shapes[key], jnp.bfloat16)
    names_out = list(out_shape)
    scratch = [pltpu.VMEM(shapes[key], jnp.bfloat16) for key in stream] + scratch
    if raw or stream or fetch:
        scratch.append(pltpu.SemaphoreType.DMA((len(stream + fetch) + len(raw),)))
    results = pl.pallas_call(
        functools.partial(stage_kernel, chips, job, list(raw), stream, fetch, names_in, names_out),
        out_shape=list(out_shape.values()),
        in_specs=[VMEM] * len(ins) + [HBM] * (len(kinds) + len(raw)),
        out_specs=[VMEM] * len(names_out),
        scratch_shapes=scratch,
        input_output_aliases={names_in.index(a): names_out.index(b) for a, b in aliases.items()},
        compiler_params=pltpu.CompilerParams(vmem_limit_bytes=LIMIT),
        cost_estimate=pl.CostEstimate(
            flops=flops, bytes_accessed=sum(2 * a * b for a, b in shapes.values()), transcendentals=0
        ),
        name=name,
    )(
        *ins.values(),
        *(pltpu.with_memory_space_constraint(x, pltpu.HBM) for x in [*(weights[k] for k in kinds), *dict(raw).values()]),
    )
    results = dict(zip(names_out, results))
    for key in fetch:
        blocks[key] = results.pop(key)
    return results


def multiply(layer, chips, shards, block, named, out):
    def add(name, value, e):
        if e:
            out[name][...] += value
        elif ("old", name) in named:
            out[name][...] = named["old", name][...] + value
        else:
            out[name][...] = value

    ys = {}
    for e, shard in enumerate(shards):
        x = named["x", shard][...].astype(jnp.float32)
        size = x.shape[1]
        square = x * x
        add("squares", sum(square[:, lane : lane + 128] for lane in range(0, size, 128)), e)
        span = pl.ds(pl.multiple_of(shard_at(*shard, chips) * size, size), size)
        ys[shard] = (x * named["gain"][layer : layer + 1, span]).astype(jnp.bfloat16)
    for name, kind in (("up", "u"), ("gate", "g")):
        for e, shard in enumerate(shards):
            add(name, jnp.dot(ys[shard], block((kind, layer, *shard)), preferred_element_type=jnp.float32), e)


def ring_body(chips, stream_in, norm_gain, w_gate, w_up, w_down):
    micro, seqs, cols = stream_in.shape
    rows = micro * seqs
    layers, features, hid = w_gate.shape
    far = chips // 2
    ring = [chip_at(place, chips) for place in range(chips)]
    right = [(2 * ring[i] + c, 2 * ring[(i + 1) % chips] + c) for i in range(chips) for c in range(2)]
    left = [(b, a) for a, b in right]
    swap = [(i, i ^ 1) for i in range(2 * chips)]
    f32, bf16 = jnp.float32, jnp.bfloat16
    weights = {"g": w_gate, "u": w_up, "d": w_down}
    blocks = {}
    kept = {}
    flops = 2 * rows * cols * hid

    def send(x, perm):
        return lax.ppermute(x, AXIS, perm)

    def fence(*groups):
        found = []

        def walk(value, visit):
            if isinstance(value, dict):
                return {key: walk(part, visit) for key, part in value.items()}
            if isinstance(value, (list, tuple)):
                return type(value)(walk(part, visit) for part in value)
            return visit(value) if isinstance(value, jax.Array) else value

        walk(groups, lambda x: found.append(x))
        kept = iter(lax.optimization_barrier(found))
        out = walk(groups, lambda x: next(kept))
        return out if len(out) > 1 else out[0]

    sums = {
        "gate": jax.ShapeDtypeStruct((rows, hid), f32),
        "up": jax.ShapeDtypeStruct((rows, hid), f32),
        "squares": jax.ShapeDtypeStruct((rows, 128), f32),
    }

    def both(offset):
        return [offset, -offset] if offset > 0 else [0] if offset == 0 else []

    stages = [[(0, False)], [(0, True), (-1, False), (1, False)]]
    stages += [[(1 - s, True), (s - 1, True), (-s, False), (s, False)] for s in range(2, far)]
    stages += [[(1 - far, True)], [(far - 1, True), (far, False)], [(far, True)]]

    units = []
    for layer in range(layers):
        units += [[("g", layer, *shard), ("u", layer, *shard)] for shards in stages for shard in shards]
        units += [[("d", layer, o, True), ("d", layer, o, False)] for step in range(far, -1, -1) for o in
                  ([far] if step == far else both(step))]
    weights["units"] = units

    def ahead(layer, name):
        return AHEAD.get((layer, name), 0)

    def shards_in(layer, xs, acc):
        ins = {"gain": kept["gain"]} if kept else {}
        ins.update({("x", shard): x for shard, x in xs.items() if kept})
        ins.update({("old", name): value for name, value in acc.items()})
        keys = [(kind, layer, *shard) for kind in "ug" for shard in xs]
        return ins, keys

    def gate_up(layer, xs, acc, fetch):
        ins, keys = shards_in(layer, xs, acc)
        outs = sums

        def job(block, named, out, scratch):
            multiply(layer, chips, list(xs), block, named, out)

        raw = {} if kept else {"gain": norm_gain, ("x", (0, False)): stream}
        out = stage(
            chips, weights, blocks, job, keys, ins, outs, {("old", name): name for name in acc}, [], fetch,
            len(keys) * flops, "gate_up", raw,
        )
        for name in raw:
            kept[name] = out.pop(name)
        return out

    def finish(layer, xs, acc, fetch):
        ins, keys = shards_in(layer, xs, acc)

        def job(block, named, out, scratch):
            into = dict(zip(sums, scratch))
            multiply(layer, chips, list(xs), block, named, into)
            meansq = jnp.sum(into["squares"][...], axis=1, keepdims=True) / features
            scale = lax.rsqrt(meansq + EPS)
            g = into["gate"][...] * scale
            hidden = (g / (1.0 + jnp.exp(-g)) * (into["up"][...] * scale)).astype(bf16)
            out["hidden"][...] = hidden
            project(layer, [far], hidden, block, out)

        outs = {"hidden": jax.ShapeDtypeStruct((rows, hid), bf16), **chunk_shapes([far])}
        scratch = [pltpu.VMEM(s.shape, s.dtype) for s in sums.values()]
        return stage(
            chips, weights, blocks, job, keys + [("d", layer, far, s) for s in (True, False)], ins, outs, {},
            scratch, fetch, (len(keys) + 2) * flops, "hidden",
        )

    def chunk_shapes(offsets):
        outs = {"sib": jax.ShapeDtypeStruct((len(offsets) * rows, cols), bf16)}
        outs.update({("own", o): jax.ShapeDtypeStruct((rows, cols), f32) for o in offsets})
        return outs

    def project(layer, offsets, hidden, block, out):
        for e, o in enumerate(offsets):
            sib = jnp.dot(hidden, block(("d", layer, o, True)), preferred_element_type=f32)
            out["sib"][e * rows : (e + 1) * rows, :] = sib.astype(bf16)
            out["own", o][...] = jnp.dot(hidden, block(("d", layer, o, False)), preferred_element_type=f32)

    def down(layer, offsets, hidden, fetch):
        def job(block, named, out, scratch):
            project(layer, offsets, named["hidden"][...], block, out)

        keys = [("d", layer, o, s) for o in offsets for s in (True, False)]
        return stage(
            chips, weights, blocks, job, keys, {"hidden": hidden}, chunk_shapes(offsets), {}, [], fetch,
            len(keys) * flops, "down",
        )

    stream = stream_in.reshape(rows, cols)
    for layer in range(layers):
        r = l = stream
        acc = {}
        held = {(0, False): stream}
        crossed = {(0, True): send(stream, swap)}
        for step in range(1, far + 1):
            r = send(r, right)
            if step < far:
                l = send(l, left)
            acc = gate_up(layer, held, acc, ahead(layer, "gather%d" % step))
            if step == far:
                l, acc, crossed = fence(l, acc, crossed)
                late = send(l, swap)
                acc = gate_up(layer, {(far - 1, False): l, **crossed}, acc, ahead(layer, "gathered"))
                r, late, acc = fence(r, late, acc)
                break
            r, acc = fence(r, acc)
            held = {**crossed, (-step, False): r}
            crossed = {(-step, True): send(r, swap)}
            if step + 1 < far:
                l, held = fence(l, held)
                held[step, False] = l
                crossed[step, True] = send(l, swap)
        crossed = {(far, True): send(r, swap)}
        acc = gate_up(layer, {(far - 1, True): late, (far, False): r}, acc, ahead(layer, "last"))
        acc, crossed = fence(acc, crossed)
        found = finish(layer, crossed, acc, ahead(layer, "hidden"))
        hidden, found = fence(found.pop("hidden"), found)
        c = send(found["sib"], swap)
        own = found["own", far]
        found = down(layer, both(far - 1), hidden, ahead(layer, "scatter%d" % far))
        c, found = fence(c, found)
        total = (own + c.astype(f32)).astype(bf16)
        hidden, total = fence(hidden, total)
        r, l = total[: rows // 2], total[rows // 2 :]
        for step in range(far - 1, -1, -1):
            r, l = send(r, right), send(l, left)
            if not step:
                if ahead(layer, "scatter0"):
                    count = ahead(layer, "scatter0")
                    stage(chips, weights, blocks, lambda *given: None, [], {"hidden": hidden}, {}, {}, [], count, 0, "ahead")
                break
            c = send(found["sib"], swap)
            own = [found["own", o] for o in both(step)]
            found = down(layer, both(step - 1), hidden, ahead(layer, "scatter%d" % step))
            l, c, found = fence(l, c, found)
            if step == far - 1:
                l = jnp.concatenate([jnp.zeros_like(l), l], 0)
            l = fence((own[1] + c[rows:].astype(f32) + l.astype(f32)).astype(bf16))
            r, _ = fence(r, l)
            if step == far - 1:
                r = jnp.concatenate([r, jnp.zeros_like(r)], 0)
            r = (own[0] + c[:rows].astype(f32) + r.astype(f32)).astype(bf16)
            hidden, r = fence(hidden, r)
            if step == 1:
                c = send(found["sib"], swap)
        r, l, c, _ = fence(r, l, c, dict(blocks))
        branch = found["own", 0] + c.astype(f32) + r.astype(f32) + l.astype(f32)
        stream = (stream.astype(f32) + branch).astype(bf16)
    return stream.reshape(micro, seqs, cols)


def plain_body(stream_in, norm_gain, w_gate, w_up, w_down):
    micro, seqs, cols = stream_in.shape
    layers = w_gate.shape[0]
    f32, bf16 = jnp.float32, jnp.bfloat16
    stream = stream_in.reshape(micro * seqs, cols)
    for layer in range(layers):
        whole = lax.all_gather(stream, AXIS, axis=1, tiled=True).astype(f32)
        meansq = jnp.mean(whole * whole, axis=1, keepdims=True)
        normed = (whole * lax.rsqrt(meansq + EPS) * norm_gain[layer]).astype(bf16)
        gate_out = jnp.dot(normed, w_gate[layer], preferred_element_type=f32)
        up_out = jnp.dot(normed, w_up[layer], preferred_element_type=f32)
        hidden = (jax.nn.silu(gate_out) * up_out).astype(bf16)
        partials = jnp.dot(hidden, w_down[layer], preferred_element_type=f32)
        branch = lax.psum_scatter(partials, AXIS, scatter_dimension=1, tiled=True)
        stream = (stream.astype(f32) + branch).astype(bf16)
    return stream.reshape(micro, seqs, cols)


def solution(mesh):
    devices = mesh.shape[AXIS]

    def body(stream_in, *rest):
        cols = stream_in.shape[2]
        if devices >= 16 and devices % 4 == 0 and cols % 128 == 0:
            return ring_body(devices // 2, stream_in, *rest)
        return plain_body(stream_in, *rest)

    return jax.shard_map(
        body,
        mesh=mesh,
        in_specs=(
            P(None, "groups", AXIS),
            P(),
            P(None, None, AXIS),
            P(None, None, AXIS),
            P(None, AXIS, None),
        ),
        out_specs=P(None, "groups", AXIS),
        check_vma=False,
    )
```
